32 devices in a mesh: dp: 2 (over x), cent: 16 (over z, y, core).
Axes of the slice: x: 2, y: 2, z: 4, core: 2. Of those that a mesh axis runs over, the one named last changes fastest.
Arguments:
- vectors: bfloat16 [512, 1024], P(('dp', 'cent')), may hold values from -16 to 16
- centroids: bfloat16 [65536, 1024], P('cent'), may hold values from -0.1125 to 0.1125
Outputs:
- new_centroids: bfloat16 [65536, 1024], P('cent', 'dp')
- loads: float32 [65536], P('cent')
The draws below stay inside these ranges and needn't reach their ends.
All inputs are finite; a program needn't handle non-finite values.
Results may differ from the reference program's by a relative error of at most 0.0075.
Values may be sent and summed in bfloat16 or wider, within the bound.
A program may use at most 128 MiB of HBM per device.

```python
import math
import jax
import jax.numpy as jnp
from jax import lax

D = 1024
K = 65536
ROW_DEV = 16
NV = 512
N_DP = 2
N_CENT = 16


def centroid_row(key, position):
    row_key = jax.random.fold_in(jax.random.fold_in(key, 7), position)
    key_noise, key_spread = jax.random.split(row_key)
    noise = jnp.clip(jax.random.normal(key_noise, (D,), jnp.float32), -6.0, 6.0)
    spread = jnp.exp(jax.random.uniform(key_spread, (), jnp.float32, math.log(0.2), math.log(0.6)))
    return noise * spread / math.sqrt(D)


def draw_centroids(key, part):
    row_ids = jnp.arange(K, dtype=jnp.int32)
    return jax.vmap(lambda position: centroid_row(key, position))(row_ids).astype(jnp.bfloat16)


def draw_vectors(key, part):
    own_key = jax.random.fold_in(key, 11)
    key_scale, key_noise = jax.random.split(own_key, 2)
    scales = jnp.exp(jax.random.uniform(key_scale, (NV, 1), jnp.float32, math.log(0.1), math.log(0.5)))
    noise = jnp.clip(jax.random.normal(key_noise, (NV, D), jnp.float32), -6.0, 6.0)
    values = noise * scales
    return values.astype(jnp.bfloat16)


def setup_inputs(seed: int = 0) -> dict:
    key_list = jax.random.split(jax.random.key(seed), 3)
    vectors = draw_vectors(jax.random.fold_in(key_list[2], 71), 0)
    centroids = draw_centroids(jax.random.fold_in(key_list[2], 71), 0)
    return dict(vectors=vectors, centroids=centroids)


softness_scale = 0.1

def reference(vectors, centroids):
    group_rows = ROW_DEV * N_CENT
    grouped = vectors.reshape(N_DP, group_rows, D)

    def accumulate(carry, collected_rows):
        sums, column_mass = carry
        logit_scores = jnp.dot(collected_rows, centroids.T, preferred_element_type=jnp.float32) / softness_scale
        highest = lax.optimization_barrier(jnp.max(logit_scores, axis=1, keepdims=True))
        exponent = jnp.exp(logit_scores - highest)
        summed = lax.optimization_barrier(jnp.sum(exponent, axis=1, keepdims=True))
        probability = exponent / summed
        weights = probability.astype(jnp.bfloat16)
        partial_value = jnp.dot(weights.T, collected_rows, preferred_element_type=jnp.float32)
        rounded = lax.optimization_barrier(partial_value.astype(jnp.bfloat16)).astype(jnp.float32)
        return ((sums + rounded, column_mass + lax.optimization_barrier(jnp.sum(probability, axis=0))), None)
    start = (jnp.zeros((K, D), jnp.float32), jnp.zeros((K,), jnp.float32))
    (sums, counts), unused = lax.scan(accumulate, start, grouped)
    mass_scale = K / (ROW_DEV * N_DP * N_CENT)
    loads = counts * mass_scale
    shifted = centroids.astype(jnp.float32) + sums * mass_scale
    factor = lax.rsqrt(lax.optimization_barrier(jnp.mean(shifted * shifted, axis=1, keepdims=True)) + 1e-06)
    new_centroids = (shifted * factor).astype(jnp.bfloat16)
    return (new_centroids, loads)
```

```python
import jax
import jax.numpy as jnp
from jax import lax
from jax.sharding import PartitionSpec as P

softness_scale = 0.1


def on_device(vectors, centroids):
    dp = lax.axis_size("dp")
    cent = lax.axis_size("cent")
    total_rows = vectors.shape[0] * dp * cent
    mass_scale = centroids.shape[0] * cent / total_rows
    rows = lax.all_gather(vectors, ("dp", "cent"), axis=0, tiled=True)
    scores = (
        lax.dot_general(
            centroids, rows, (((1,), (1,)), ((), ())), preferred_element_type=jnp.float32
        )
        / softness_scale
    )
    local_peak = jnp.max(scores, axis=0)
    exponent = jnp.exp(scores - local_peak[None, :])
    local_sum = jnp.sum(exponent, axis=0)
    stats = lax.all_gather(jnp.stack([local_peak, local_sum]), "cent", axis=0)
    highest = jnp.max(stats[:, 0], axis=0)
    summed = jnp.sum(stats[:, 1] * jnp.exp(stats[:, 0] - highest[None, :]), axis=0)
    rescale = jnp.exp(local_peak - highest) / summed
    probability = exponent * rescale[None, :]
    weights = probability.astype(jnp.bfloat16)
    loads = jnp.sum(probability, axis=1) * mass_scale
    sums = lax.dot_general(
        weights, rows, (((1,), (0,)), ((), ())), preferred_element_type=jnp.float32
    )
    shifted = centroids.astype(jnp.float32) + sums * mass_scale
    factor = lax.rsqrt(jnp.mean(shifted * shifted, axis=1, keepdims=True) + 1e-06)
    columns = centroids.shape[1] // dp
    own = lax.dynamic_slice_in_dim(shifted, lax.axis_index("dp") * columns, columns, 1)
    return ((own * factor).astype(jnp.bfloat16), loads)


def solution(mesh):
    placed = (P(("dp", "cent"), None), P("cent", None))
    return jax.shard_map(
        on_device,
        mesh=mesh,
        in_specs=placed,
        out_specs=(P("cent", "dp"), P("cent")),
        check_vma=False,
    )
```

```python
import functools
import math
import jax
import jax.numpy as jnp
from jax import lax
from jax.experimental import pallas as pl
from jax.experimental.pallas import tpu as pltpu
from jax.sharding import PartitionSpec as P

softness_scale = 0.1
MESH = pl.DeviceIdType.MESH
LANES = 128
SCORE_ROWS = 1024
SUM_ROWS = 512
EXP_ROWS = 64
VMEM_BYTES = 56 * 1024 * 1024


def plain_form(vectors, centroids):
    dp = lax.axis_size("dp")
    cent = lax.axis_size("cent")
    total_rows = vectors.shape[0] * dp * cent
    mass_scale = centroids.shape[0] * cent / total_rows
    rows = lax.all_gather(vectors, ("dp", "cent"), axis=0, tiled=True)
    scores = (
        lax.dot_general(
            centroids, rows, (((1,), (1,)), ((), ())), preferred_element_type=jnp.float32
        )
        / softness_scale
    )
    local_peak = jnp.max(scores, axis=0)
    exponent = jnp.exp(scores - local_peak[None, :])
    local_sum = jnp.sum(exponent, axis=0)
    stats = lax.all_gather(jnp.stack([local_peak, local_sum]), "cent", axis=0)
    highest = jnp.max(stats[:, 0], axis=0)
    summed = jnp.sum(stats[:, 1] * jnp.exp(stats[:, 0] - highest[None, :]), axis=0)
    rescale = jnp.exp(local_peak - highest) / summed
    probability = exponent * rescale[None, :]
    weights = probability.astype(jnp.bfloat16)
    loads = jnp.sum(probability, axis=1) * mass_scale
    sums = lax.dot_general(
        weights, rows, (((1,), (0,)), ((), ())), preferred_element_type=jnp.float32
    )
    shifted = centroids.astype(jnp.float32) + sums * mass_scale
    factor = lax.rsqrt(jnp.mean(shifted * shifted, axis=1, keepdims=True) + 1e-06)
    columns = centroids.shape[1] // dp
    own = lax.dynamic_slice_in_dim(shifted, lax.axis_index("dp") * columns, columns, 1)
    return ((own * factor).astype(jnp.bfloat16), loads)


def gather_kernel(
    cent, nz, vec_hbm, cen_hbm, e_hbm, rows_hbm, resc_ref,
    cen, scores, expo, rows, stats,
    local_sem, cen_sem, out_sem, send_sem, recv_sem, sib_send, sib_recv, stat_send, stat_recv,
):
    x = lax.axis_index("dp")
    i = lax.axis_index("cent")
    c = i % 2
    y = (i // 2) % 2
    z = i // 4

    chunks = cen_hbm.shape[0] // SCORE_ROWS

    def cen_copy(j):
        span = pl.ds(pl.multiple_of(j * SCORE_ROWS, SCORE_ROWS), SCORE_ROWS)
        return pltpu.make_async_copy(cen_hbm.at[span], cen.at[span], cen_sem.at[j])

    own0 = (z * 2 + y) * 2 + x
    own1 = (x * 2 + y) * nz + z
    own = jnp.where(c == 0, own0, own1)
    mine = pltpu.make_async_copy(vec_hbm, rows.at[c, own], local_sem.at[0])
    mine.start()
    for j in range(chunks):
        cen_copy(j).start()

    barrier = pltpu.get_barrier_semaphore()
    for o in range(1, cent):
        pl.semaphore_signal(
            barrier, inc=1, device_id=(x, lax.rem(i + o, cent)), device_id_type=MESH
        )
    pl.semaphore_signal(barrier, inc=1, device_id=(1 - x, i), device_id_type=MESH)
    mine.wait()
    pl.semaphore_wait(barrier, cent)

    def at(zz, yy, cc):
        return (zz * 2 + yy) * 2 + cc

    def send(core, start, count, to, send_at, recv_at):
        piece = rows.at[core, pl.ds(start, count)]
        return pltpu.make_async_remote_copy(
            src_ref=piece, dst_ref=piece, send_sem=send_sem.at[send_at],
            recv_sem=recv_sem.at[recv_at], device_id=to, device_id_type=MESH,
        )

    def sibling(core, start, count, slot):
        piece = rows.at[core, pl.ds(start, count)]
        return pltpu.make_async_remote_copy(
            src_ref=piece, dst_ref=piece, send_sem=sib_send.at[slot],
            recv_sem=sib_recv.at[slot], device_id=(x, at(z, y, 1 - core)), device_id_type=MESH,
        )

    def along_z(core, first, count, visit):
        def up(zz):
            return send(core, first(zz), count, (x, at(z + 1, y, core)), 2 + zz, 2 + zz)

        def down(zz):
            return send(core, first(zz), count, (x, at(z - 1, y, core)), 2 + nz + zz, 2 + zz)

        for s in range(nz):
            @pl.when(z - s >= 0)
            def _():
                if s:
                    up(z - s).wait_recv()

                @pl.when(z < nz - 1)
                def _():
                    up(z - s).start()

                visit(z - s)

            if s:
                @pl.when(z + s < nz)
                def _():
                    down(z + s).wait_recv()

            @pl.when(jnp.logical_and(z + s < nz, z > 0))
            def _():
                down(z + s).start()

            if s:
                @pl.when(z + s < nz)
                def _():
                    visit(z + s)

        def drain():
            for s in range(nz):
                @pl.when(jnp.logical_and(z - s >= 0, z < nz - 1))
                def _():
                    up(z - s).wait_send()

                @pl.when(jnp.logical_and(z + s < nz, z > 0))
                def _():
                    down(z + s).wait_send()

        return drain

    @pl.when(c == 0)
    def _():
        over_x = send(0, own0, 1, (1 - x, i), 0, 0)
        over_x.start()
        over_x.wait_recv()
        over_y = send(0, (z * 2 + y) * 2, 2, (x, at(z, 1 - y, 0)), 1, 1)
        over_y.start()
        over_y.wait_recv()
        drain = along_z(
            0, lambda zz: zz * 4, 4, lambda zz: sibling(0, zz * 4, 4, zz).start()
        )
        over_x.wait_send()
        over_y.wait_send()
        drain()
        for zz in range(nz):
            sibling(0, zz * 4, 4, zz).wait_send()
        for h in range(2):
            sibling(1, h * 2 * nz, 2 * nz, h).wait_recv()

    @pl.when(c == 1)
    def _():
        drain = along_z(1, lambda zz: (x * 2 + y) * nz + zz, 1, lambda zz: None)
        over_y = send(1, (x * 2 + y) * nz, nz, (x, at(z, 1 - y, 1)), 1, 1)
        over_y.start()
        over_y.wait_recv()
        over_x = send(1, x * 2 * nz, 2 * nz, (1 - x, i), 0, 0)
        over_x.start()
        sibling(1, x * 2 * nz, 2 * nz, x).start()
        over_x.wait_recv()
        sibling(1, (1 - x) * 2 * nz, 2 * nz, 1 - x).start()
        over_x.wait_send()
        over_y.wait_send()
        drain()
        for h in range(2):
            sibling(1, h * 2 * nz, 2 * nz, h).wait_send()
        for zz in range(nz):
            sibling(0, zz * 4, 4, zz).wait_recv()

    total = rows.shape[0] * rows.shape[1] * rows.shape[2]
    rows_out = pltpu.make_async_copy(rows, rows_hbm, local_sem.at[1])
    rows_out.start()
    everything = rows[...].reshape(total, rows.shape[3])

    def score(j, peak):
        cen_copy(j).wait()
        span = pl.ds(pl.multiple_of(j * SCORE_ROWS, SCORE_ROWS), SCORE_ROWS)
        block = lax.dot_general(
            cen[span], everything, (((1,), (1,)), ((), ())), preferred_element_type=jnp.float32
        )
        scores[span] = block
        return jnp.maximum(peak, jnp.max(block.reshape(-1, 8, total), axis=0))

    peak = lax.fori_loop(0, chunks, score, jnp.full((8, total), -jnp.inf, jnp.float32))
    peak = jnp.max(peak, axis=0, keepdims=True)
    scale = math.log2(math.e) / softness_scale

    def e_copy(j):
        span = pl.ds(pl.multiple_of(j * SCORE_ROWS, SCORE_ROWS), SCORE_ROWS)
        return pltpu.make_async_copy(expo.at[span], e_hbm.at[span], out_sem.at[j])

    def exponents(j, acc):
        def part(t, acc):
            span = pl.ds(pl.multiple_of(j * SCORE_ROWS + t * EXP_ROWS, EXP_ROWS), EXP_ROWS)
            value = jnp.exp2((scores[span] - peak) * scale)
            expo[span] = value.astype(jnp.bfloat16)
            return acc + jnp.sum(value.reshape(-1, 8, total), axis=0)

        acc = lax.fori_loop(0, SCORE_ROWS // EXP_ROWS, part, acc)
        e_copy(j).start()
        return acc

    acc = lax.fori_loop(0, chunks, exponents, jnp.zeros((8, total), jnp.float32))
    acc = jnp.sum(acc, axis=0, keepdims=True)

    groups = total // LANES
    for g in range(groups):
        stats[i, g : g + 1, :] = peak[:, g * LANES : (g + 1) * LANES]
        stats[i, groups + g : groups + g + 1, :] = acc[:, g * LANES : (g + 1) * LANES]

    def stat_copy(o):
        return pltpu.make_async_remote_copy(
            src_ref=stats.at[i], dst_ref=stats.at[i], send_sem=stat_send.at[o],
            recv_sem=stat_recv.at[o], device_id=(x, lax.rem(i + o, cent)), device_id_type=MESH,
        )

    for o in range(1, cent):
        stat_copy(o).start()
    for o in range(1, cent):
        pltpu.make_async_remote_copy(
            src_ref=stats.at[i], dst_ref=stats.at[lax.rem(i + cent - o, cent)],
            send_sem=stat_send.at[o], recv_sem=stat_recv.at[o],
            device_id=(x, lax.rem(i + o, cent)), device_id_type=MESH,
        ).wait_recv()
    peaks = stats[:, 0:groups, :]
    highest = jnp.max(peaks, axis=0)
    summed = jnp.sum(stats[:, groups : 2 * groups, :] * jnp.exp2((peaks - highest) * scale), axis=0)
    resc_ref[...] = jnp.exp2((stats[i, 0:groups, :] - highest) * scale) / summed
    for o in range(1, cent):
        stat_copy(o).wait_send()
    rows_out.wait()
    for j in range(chunks):
        e_copy(j).wait()


def update_kernel(
    mass_scale, which, e_ref, resc_ref, cen_own, cen_other, rows_own, rows_other, new_ref, loads_ref
):
    j = pl.program_id(0)
    groups = resc_ref.shape[0]
    mass = None
    parts = []
    for g in range(groups):
        lanes = slice(g * LANES, (g + 1) * LANES)
        p = e_ref[:, lanes].astype(jnp.float32) * resc_ref[g : g + 1, :]
        mass = p if mass is None else mass + p
        parts.append(p.astype(jnp.bfloat16))
    weights = jnp.concatenate(parts, axis=1)
    for b in range(mass.shape[0] // LANES):
        block = mass[b * LANES : (b + 1) * LANES].T
        loads_ref[j, b : b + 1, :] = jnp.sum(block, axis=0, keepdims=True) * mass_scale
    own = cen_own[...].astype(jnp.float32) + mass_scale * jnp.dot(
        weights, rows_own[...], preferred_element_type=jnp.float32
    )
    other = cen_other[...].astype(jnp.float32) + mass_scale * jnp.dot(
        weights, rows_other[...], preferred_element_type=jnp.float32
    )
    width = own.shape[1] + other.shape[1]
    square = (
        jnp.sum(own * own, axis=1, keepdims=True) + jnp.sum(other * other, axis=1, keepdims=True)
    ) / width
    new_ref[...] = (own * lax.rsqrt(square + 1e-06)).astype(new_ref.dtype)


def kernel_form(vectors, centroids):
    dp = lax.axis_size("dp")
    cent = lax.axis_size("cent")
    nz = cent // 4
    block_rows, width = vectors.shape
    total = block_rows * dp * cent
    local = centroids.shape[0]
    mass_scale = local * cent / total
    chunks = local // SCORE_ROWS
    groups = total // LANES
    e, rows, resc = pl.pallas_call(
        functools.partial(gather_kernel, cent, nz),
        out_shape=(
            jax.ShapeDtypeStruct((local, total), jnp.bfloat16),
            jax.ShapeDtypeStruct((2, 4 * nz, block_rows, width), jnp.bfloat16),
            jax.ShapeDtypeStruct((groups, LANES), jnp.float32),
        ),
        in_specs=[pl.BlockSpec(memory_space=pl.ANY)] * 2,
        out_specs=(
            pl.BlockSpec(memory_space=pl.ANY),
            pl.BlockSpec(memory_space=pl.ANY),
            pl.BlockSpec(memory_space=pltpu.VMEM),
        ),
        scratch_shapes=[
            pltpu.VMEM((local, width), jnp.bfloat16),
            pltpu.VMEM((local, total), jnp.float32),
            pltpu.VMEM((local, total), jnp.bfloat16),
            pltpu.VMEM((2, 4 * nz, block_rows, width), jnp.bfloat16),
            pltpu.VMEM((cent, 2 * groups, LANES), jnp.float32),
            pltpu.SemaphoreType.DMA((2,)),
            pltpu.SemaphoreType.DMA((chunks,)),
            pltpu.SemaphoreType.DMA((chunks,)),
            pltpu.SemaphoreType.DMA((2 + 2 * nz,)),
            pltpu.SemaphoreType.DMA((2 + nz,)),
            pltpu.SemaphoreType.DMA((nz,)),
            pltpu.SemaphoreType.DMA((nz,)),
            pltpu.SemaphoreType.DMA((cent,)),
            pltpu.SemaphoreType.DMA((cent,)),
        ],
        compiler_params=pltpu.CompilerParams(
            collective_id=0, has_side_effects=True, vmem_limit_bytes=VMEM_BYTES
        ),
        cost_estimate=pl.CostEstimate(
            flops=2 * local * total * width, bytes_accessed=2 * local * (width + total),
            transcendentals=local * total,
        ),
    )(vectors, centroids)
    rows = rows.reshape(total, width)
    half = width // 2
    steps = local // SUM_ROWS
    which = jnp.reshape(lax.axis_index("dp"), (1,)).astype(jnp.int32)
    new, loads = pl.pallas_call(
        functools.partial(update_kernel, mass_scale),
        out_shape=(
            jax.ShapeDtypeStruct((local, half), jnp.bfloat16),
            jax.ShapeDtypeStruct((steps, SUM_ROWS // LANES, LANES), jnp.float32),
        ),
        grid_spec=pltpu.PrefetchScalarGridSpec(
            num_scalar_prefetch=1,
            grid=(steps,),
            in_specs=[
                pl.BlockSpec((SUM_ROWS, total), lambda j, d: (j, 0)),
                pl.BlockSpec((groups, LANES), lambda j, d: (0, 0)),
                pl.BlockSpec((SUM_ROWS, half), lambda j, d: (j, d[0])),
                pl.BlockSpec((SUM_ROWS, half), lambda j, d: (j, 1 - d[0])),
                pl.BlockSpec((total, half), lambda j, d: (0, d[0])),
                pl.BlockSpec((total, half), lambda j, d: (0, 1 - d[0])),
            ],
            out_specs=(
                pl.BlockSpec((SUM_ROWS, half), lambda j, d: (j, 0)),
                pl.BlockSpec((steps, SUM_ROWS // LANES, LANES), lambda j, d: (0, 0, 0)),
            ),
        ),
        compiler_params=pltpu.CompilerParams(vmem_limit_bytes=VMEM_BYTES),
        cost_estimate=pl.CostEstimate(
            flops=2 * local * total * width, bytes_accessed=2 * local * (width + total + half),
            transcendentals=local,
        ),
    )(which, e, resc, centroids, centroids, rows, rows)
    return (new, loads.reshape(local))


def solution(mesh):
    dp, cent = mesh.shape["dp"], mesh.shape["cent"]

    def on_device(vectors, centroids):
        total = vectors.shape[0] * dp * cent
        fits = (
            dp == 2
            and cent % 4 == 0
            and cent >= 8
            and vectors.shape[0] % 16 == 0
            and total % LANES == 0
            and total <= 1024
            and centroids.shape[0] % SCORE_ROWS == 0
            and centroids.shape[0] <= 4096
        )
        return (kernel_form if fits else plain_form)(vectors, centroids)

    placed = (P(("dp", "cent"), None), P("cent", None))
    return jax.shard_map(
        on_device,
        mesh=mesh,
        in_specs=placed,
        out_specs=(P("cent", "dp"), P("cent")),
        check_vma=False,
    )
```

```python
import functools
import math
import jax
import jax.numpy as jnp
from jax import lax
from jax.experimental import pallas as pl
from jax.experimental.pallas import tpu as pltpu
from jax.sharding import PartitionSpec as P

softness_scale = 0.1
MESH = pl.DeviceIdType.MESH
LANES = 128
SCORE_ROWS = 1024
SUM_ROWS = 1024
EXP_ROWS = 64
VMEM_BYTES = 56 * 1024 * 1024


def plain_form(vectors, centroids):
    dp = lax.axis_size("dp")
    cent = lax.axis_size("cent")
    total_rows = vectors.shape[0] * dp * cent
    mass_scale = centroids.shape[0] * cent / total_rows
    rows = lax.all_gather(vectors, ("dp", "cent"), axis=0, tiled=True)
    scores = (
        lax.dot_general(
            centroids, rows, (((1,), (1,)), ((), ())), preferred_element_type=jnp.float32
        )
        / softness_scale
    )
    local_peak = jnp.max(scores, axis=0)
    exponent = jnp.exp(scores - local_peak[None, :])
    local_sum = jnp.sum(exponent, axis=0)
    stats = lax.all_gather(jnp.stack([local_peak, local_sum]), "cent", axis=0)
    highest = jnp.max(stats[:, 0], axis=0)
    summed = jnp.sum(stats[:, 1] * jnp.exp(stats[:, 0] - highest[None, :]), axis=0)
    rescale = jnp.exp(local_peak - highest) / summed
    probability = exponent * rescale[None, :]
    weights = probability.astype(jnp.bfloat16)
    loads = jnp.sum(probability, axis=1) * mass_scale
    sums = lax.dot_general(
        weights, rows, (((1,), (0,)), ((), ())), preferred_element_type=jnp.float32
    )
    shifted = centroids.astype(jnp.float32) + sums * mass_scale
    factor = lax.rsqrt(jnp.mean(shifted * shifted, axis=1, keepdims=True) + 1e-06)
    columns = centroids.shape[1] // dp
    own = lax.dynamic_slice_in_dim(shifted, lax.axis_index("dp") * columns, columns, 1)
    return ((own * factor).astype(jnp.bfloat16), loads)


def gather_kernel(
    cent, nz, mass_scale, vec_hbm, cen_hbm, e_hbm, rows_hbm, resc_ref,
    cen, scores, expo, rows, stats, resc,
    local_sem, cen_sem, out_sem, z_send, z_recv, xy_send, xy_recv, relay_send, relay_recv,
    sib_send, sib_recv, stat_send, stat_recv,
):
    x = lax.axis_index("dp")
    i = lax.axis_index("cent")
    c = i % 2
    y = (i // 2) % 2
    z = i // 4
    total = scores.shape[1]
    pair = 2 * LANES
    chunks = cen_hbm.shape[0] // SCORE_ROWS

    def chunk_span(j):
        return pl.ds(pl.multiple_of(j * SCORE_ROWS, SCORE_ROWS), SCORE_ROWS)

    def cen_copy(j):
        return pltpu.make_async_copy(
            cen_hbm.at[chunk_span(j)], cen.at[chunk_span(j)], cen_sem.at[j]
        )

    own = x * 2 + y
    mine = pltpu.make_async_copy(vec_hbm, rows.at[z, c, own], local_sem.at[0])
    mine.start()
    for j in range(chunks):
        cen_copy(j).start()

    barrier = pltpu.get_barrier_semaphore()
    for o in range(1, cent):
        pl.semaphore_signal(
            barrier, inc=1, device_id=(x, lax.rem(i + o, cent)), device_id_type=MESH
        )
    pl.semaphore_signal(barrier, inc=1, device_id=(1 - x, i), device_id_type=MESH)
    mine.wait()
    pl.semaphore_wait(barrier, cent)

    def slab(o):
        return lax.rem(z + nz - o, nz)

    def remote(piece, send_sem, recv_sem, to):
        return pltpu.make_async_remote_copy(
            src_ref=piece, dst_ref=piece, send_sem=send_sem, recv_sem=recv_sem,
            device_id=to, device_id_type=MESH,
        )

    x_peer = (1 - x, i)
    y_peer = (x, (z * 2 + 1 - y) * 2 + c)

    def over_z(o):
        to = (x, (lax.rem(z + o, nz) * 2 + y) * 2 + c)
        return remote(rows.at[z, c, own], z_send.at[o], z_recv.at[o], to)

    def over_x(o):
        return remote(rows.at[slab(o), c, own], xy_send.at[0, o], xy_recv.at[0, o], x_peer)

    def over_y(o):
        return remote(rows.at[slab(o), c, own], xy_send.at[1, o], xy_recv.at[1, o], y_peer)

    def arrived(way, o):
        source = jnp.where(way == 0, (1 - x) * 2 + y, x * 2 + 1 - y)
        piece = rows.at[slab(o), c, source]
        return remote(piece, xy_send.at[way, o], xy_recv.at[way, o], x_peer)

    relay_source = jnp.where(c == 0, (1 - x) * 2 + y, x * 2 + 1 - y)
    relay_to = (jnp.where(c == 0, x, 1 - x), jnp.where(c == 0, y_peer[1], i))

    def relay(o):
        return remote(
            rows.at[slab(o), c, relay_source], relay_send.at[o], relay_recv.at[o], relay_to
        )

    def relayed(o):
        piece = rows.at[slab(o), c, (1 - x) * 2 + 1 - y]
        return remote(piece, relay_send.at[o], relay_recv.at[o], relay_to)

    def sibling(o, core):
        to = (x, i + 1 - 2 * c)
        return remote(rows.at[slab(o), core], sib_send.at[o], sib_recv.at[o], to)

    def z_arrival(o):
        piece = rows.at[slab(o), c, own]
        return remote(piece, z_send.at[o], z_recv.at[o], y_peer)

    def forward(o):
        if o:
            z_arrival(o).wait_recv()
        over_x(o).start()
        over_y(o).start()

    def pass_on(o):
        arrived(c, o).wait_recv()
        relay(o).start()

    def complete(o):
        arrived(1 - c, o).wait_recv()
        relayed(o).wait_recv()
        sibling(o, c).start()

    def rows_copy(o):
        return pltpu.make_async_copy(rows.at[slab(o)], rows_hbm.at[o], local_sem.at[1 + o])

    def usable(o):
        sibling(o, 1 - c).wait_recv()
        rows_copy(o).start()

    forward(0)
    for o in range(1, nz):
        over_z(o).start()
    for o in range(1, nz):
        forward(o)
        pass_on(o - 1)
    complete(0)
    complete(1)

    def score(p, j, peak):
        if p == 0:
            cen_copy(j).wait()
        two = [rows[slab(2 * p + t)].reshape(LANES, rows.shape[4]) for t in range(2)]
        block = lax.dot_general(
            cen[chunk_span(j)], jnp.concatenate(two, axis=0), (((1,), (1,)), ((), ())),
            preferred_element_type=jnp.float32,
        )
        scores[chunk_span(j), p * pair : (p + 1) * pair] = block
        return jnp.maximum(peak, jnp.max(block.reshape(-1, 8, pair), axis=0))

    scale = math.log2(math.e) / softness_scale

    def e_copy(j):
        return pltpu.make_async_copy(
            expo.at[chunk_span(j)], e_hbm.at[chunk_span(j)], out_sem.at[j]
        )

    def exponents(p, peak, last):
        columns = slice(p * pair, (p + 1) * pair)

        def whole(j, acc):
            def part(t, acc):
                span = pl.ds(pl.multiple_of(j * SCORE_ROWS + t * EXP_ROWS, EXP_ROWS), EXP_ROWS)
                value = jnp.exp2((scores[span, columns] - peak) * scale)
                expo[span, columns] = value.astype(jnp.bfloat16)
                return acc + jnp.sum(value.reshape(-1, 8, pair), axis=0)

            acc = lax.fori_loop(0, SCORE_ROWS // EXP_ROWS, part, acc)
            if last:
                e_copy(j).start()
            return acc

        acc = lax.fori_loop(0, chunks, whole, jnp.zeros((8, pair), jnp.float32))
        acc = jnp.sum(acc, axis=0, keepdims=True)
        for t in range(2):
            lanes = slice(t * LANES, (t + 1) * LANES)
            at = slab(2 * p + t)
            stats[i, pl.ds(at, 1), :] = peak[:, lanes]
            stats[i, pl.ds(nz + at, 1), :] = acc[:, lanes]

    later = [functools.partial(pass_on, nz - 1)]
    later += [functools.partial(complete, o) for o in range(2, nz)]
    for p in range(nz // 2):
        for t in range(2):
            usable(2 * p + t)
        peak = jnp.full((8, pair), -jnp.inf, jnp.float32)
        for j in range(chunks):
            peak = score(p, j, peak)
            if later:
                later.pop(0)()
        while later:
            later.pop(0)()
        peak = jnp.max(peak, axis=0, keepdims=True)
        exponents(p, peak, p == nz // 2 - 1)

    def stat_copy(o, slot):
        return pltpu.make_async_remote_copy(
            src_ref=stats.at[i], dst_ref=stats.at[slot], send_sem=stat_send.at[o],
            recv_sem=stat_recv.at[o], device_id=(x, lax.rem(i + o, cent)), device_id_type=MESH,
        )

    for o in range(1, cent):
        stat_copy(o, i).start()
    for o in range(1, cent):
        stat_copy(o, lax.rem(i + cent - o, cent)).wait_recv()
    peaks = stats[:, 0:nz, :]
    highest = jnp.max(peaks, axis=0)
    summed = jnp.sum(stats[:, nz : 2 * nz, :] * jnp.exp2((peaks - highest) * scale), axis=0)
    resc[...] = jnp.exp2((stats[i, 0:nz, :] - highest) * scale) * (mass_scale / summed)
    for o in range(nz):
        resc_ref[o : o + 1, :] = resc[pl.ds(slab(o), 1), :]
    for o in range(1, cent):
        stat_copy(o, i).wait_send()
    for o in range(nz):
        if o:
            over_z(o).wait_send()
        over_x(o).wait_send()
        over_y(o).wait_send()
        relay(o).wait_send()
        sibling(o, c).wait_send()
        rows_copy(o).wait()
    for j in range(chunks):
        e_copy(j).wait()


def update_kernel(
    which, e_ref, resc_ref, cen_own, cen_other, rows_own, rows_other, new_ref, loads_ref
):
    j = pl.program_id(0)
    groups = resc_ref.shape[0]
    mass = None
    parts = []
    for g in range(groups):
        lanes = slice(g * LANES, (g + 1) * LANES)
        p = e_ref[:, lanes].astype(jnp.float32) * resc_ref[g : g + 1, :]
        mass = p if mass is None else mass + p
        parts.append(p.astype(jnp.bfloat16))
    weights = jnp.concatenate(parts, axis=1)
    for b in range(mass.shape[0] // LANES):
        block = mass[b * LANES : (b + 1) * LANES].T
        loads_ref[j, b : b + 1, :] = jnp.sum(block, axis=0, keepdims=True)
    own = cen_own[...].astype(jnp.float32) + jnp.dot(
        weights, rows_own[...], preferred_element_type=jnp.float32
    )
    other = cen_other[...].astype(jnp.float32) + jnp.dot(
        weights, rows_other[...], preferred_element_type=jnp.float32
    )
    width = own.shape[1] + other.shape[1]
    square = (
        jnp.sum(own * own, axis=1, keepdims=True) + jnp.sum(other * other, axis=1, keepdims=True)
    ) / width
    new_ref[...] = (own * lax.rsqrt(square + 1e-06)).astype(new_ref.dtype)


def kernel_form(vectors, centroids):
    dp = lax.axis_size("dp")
    cent = lax.axis_size("cent")
    nz = cent // 4
    block_rows, width = vectors.shape
    total = block_rows * dp * cent
    local = centroids.shape[0]
    mass_scale = local * cent / total
    chunks = local // SCORE_ROWS
    groups = total // LANES
    e, rows, resc = pl.pallas_call(
        functools.partial(gather_kernel, cent, nz, mass_scale),
        out_shape=(
            jax.ShapeDtypeStruct((local, total), jnp.bfloat16),
            jax.ShapeDtypeStruct((nz, 2, 4, block_rows, width), jnp.bfloat16),
            jax.ShapeDtypeStruct((groups, LANES), jnp.float32),
        ),
        in_specs=[pl.BlockSpec(memory_space=pl.ANY)] * 2,
        out_specs=(
            pl.BlockSpec(memory_space=pl.ANY),
            pl.BlockSpec(memory_space=pl.ANY),
            pl.BlockSpec(memory_space=pltpu.VMEM),
        ),
        scratch_shapes=[
            pltpu.VMEM((local, width), jnp.bfloat16),
            pltpu.VMEM((local, total), jnp.float32),
            pltpu.VMEM((local, total), jnp.bfloat16),
            pltpu.VMEM((nz, 2, 4, block_rows, width), jnp.bfloat16),
            pltpu.VMEM((cent, 2 * groups, LANES), jnp.float32),
            pltpu.VMEM((groups, LANES), jnp.float32),
            pltpu.SemaphoreType.DMA((1 + nz,)),
            pltpu.SemaphoreType.DMA((chunks,)),
            pltpu.SemaphoreType.DMA((chunks,)),
            pltpu.SemaphoreType.DMA((nz,)),
            pltpu.SemaphoreType.DMA((nz,)),
            pltpu.SemaphoreType.DMA((2, nz)),
            pltpu.SemaphoreType.DMA((2, nz)),
            pltpu.SemaphoreType.DMA((nz,)),
            pltpu.SemaphoreType.DMA((nz,)),
            pltpu.SemaphoreType.DMA((nz,)),
            pltpu.SemaphoreType.DMA((nz,)),
            pltpu.SemaphoreType.DMA((cent,)),
            pltpu.SemaphoreType.DMA((cent,)),
        ],
        compiler_params=pltpu.CompilerParams(
            collective_id=0, has_side_effects=True, vmem_limit_bytes=VMEM_BYTES
        ),
        cost_estimate=pl.CostEstimate(
            flops=2 * local * total * width, bytes_accessed=2 * local * (width + total),
            transcendentals=local * total,
        ),
    )(vectors, centroids)
    rows = rows.reshape(total, width)
    half = width // 2
    steps = local // SUM_ROWS
    which = jnp.reshape(lax.axis_index("dp"), (1,)).astype(jnp.int32)
    new, loads = pl.pallas_call(
        update_kernel,
        out_shape=(
            jax.ShapeDtypeStruct((local, half), jnp.bfloat16),
            jax.ShapeDtypeStruct((steps, SUM_ROWS // LANES, LANES), jnp.float32),
        ),
        grid_spec=pltpu.PrefetchScalarGridSpec(
            num_scalar_prefetch=1,
            grid=(steps,),
            in_specs=[
                pl.BlockSpec((SUM_ROWS, total), lambda j, d: (j, 0)),
                pl.BlockSpec((groups, LANES), lambda j, d: (0, 0)),
                pl.BlockSpec((SUM_ROWS, half), lambda j, d: (j, d[0])),
                pl.BlockSpec((SUM_ROWS, half), lambda j, d: (j, 1 - d[0])),
                pl.BlockSpec((total, half), lambda j, d: (0, d[0])),
                pl.BlockSpec((total, half), lambda j, d: (0, 1 - d[0])),
            ],
            out_specs=(
                pl.BlockSpec((SUM_ROWS, half), lambda j, d: (j, 0)),
                pl.BlockSpec((steps, SUM_ROWS // LANES, LANES), lambda j, d: (0, 0, 0)),
            ),
        ),
        compiler_params=pltpu.CompilerParams(vmem_limit_bytes=VMEM_BYTES),
        cost_estimate=pl.CostEstimate(
            flops=2 * local * total * width, bytes_accessed=2 * local * (width + total + half),
            transcendentals=local,
        ),
    )(which, e, resc, centroids, centroids, rows, rows)
    return (new, loads.reshape(local))


def solution(mesh):
    dp, cent = mesh.shape["dp"], mesh.shape["cent"]

    def on_device(vectors, centroids):
        total = vectors.shape[0] * dp * cent
        fits = (
            dp == 2
            and cent % 8 == 0
            and vectors.shape[0] * 8 == LANES
            and total <= 1024
            and centroids.shape[0] % SCORE_ROWS == 0
            and centroids.shape[0] <= 4096
        )
        return (kernel_form if fits else plain_form)(vectors, centroids)

    placed = (P(("dp", "cent"), None), P("cent", None))
    return jax.shard_map(
        on_device,
        mesh=mesh,
        in_specs=placed,
        out_specs=(P("cent", "dp"), P("cent")),
        check_vma=False,
    )
```

```python
import functools
import math
import jax
import jax.numpy as jnp
from jax import lax
from jax.experimental import pallas as pl
from jax.experimental.pallas import tpu as pltpu
from jax.sharding import PartitionSpec as P

softness_scale = 0.1
MESH = pl.DeviceIdType.MESH
LANES = 128
SCORE_ROWS = 1024
SUM_ROWS = 1024
EXP_ROWS = 64
VMEM_BYTES = 56 * 1024 * 1024


def plain_form(vectors, centroids):
    dp = lax.axis_size("dp")
    cent = lax.axis_size("cent")
    total_rows = vectors.shape[0] * dp * cent
    mass_scale = centroids.shape[0] * cent / total_rows
    rows = lax.all_gather(vectors, ("dp", "cent"), axis=0, tiled=True)
    scores = (
        lax.dot_general(
            centroids, rows, (((1,), (1,)), ((), ())), preferred_element_type=jnp.float32
        )
        / softness_scale
    )
    local_peak = jnp.max(scores, axis=0)
    exponent = jnp.exp(scores - local_peak[None, :])
    local_sum = jnp.sum(exponent, axis=0)
    stats = lax.all_gather(jnp.stack([local_peak, local_sum]), "cent", axis=0)
    highest = jnp.max(stats[:, 0], axis=0)
    summed = jnp.sum(stats[:, 1] * jnp.exp(stats[:, 0] - highest[None, :]), axis=0)
    rescale = jnp.exp(local_peak - highest) / summed
    probability = exponent * rescale[None, :]
    weights = probability.astype(jnp.bfloat16)
    loads = jnp.sum(probability, axis=1) * mass_scale
    sums = lax.dot_general(
        weights, rows, (((1,), (0,)), ((), ())), preferred_element_type=jnp.float32
    )
    shifted = centroids.astype(jnp.float32) + sums * mass_scale
    factor = lax.rsqrt(jnp.mean(shifted * shifted, axis=1, keepdims=True) + 1e-06)
    columns = centroids.shape[1] // dp
    own = lax.dynamic_slice_in_dim(shifted, lax.axis_index("dp") * columns, columns, 1)
    return ((own * factor).astype(jnp.bfloat16), loads)


def gather_kernel(
    cent, nz, mass_scale, vec_hbm, cen_hbm, e_hbm, rows_hbm, resc_ref,
    cen, scores, expo, rows, stats, resc,
    local_sem, cen_sem, out_sem, z_send, z_recv, xy_send, xy_recv, relay_send, relay_recv,
    sib_send, sib_recv, stat_send, stat_recv,
):
    x = lax.axis_index("dp")
    i = lax.axis_index("cent")
    c = i % 2
    y = (i // 2) % 2
    z = i // 4
    total = scores.shape[1]
    pair = total // 2
    per = pair // LANES
    chunks = cen_hbm.shape[0] // SCORE_ROWS

    def chunk_span(j):
        return pl.ds(pl.multiple_of(j * SCORE_ROWS, SCORE_ROWS), SCORE_ROWS)

    def cen_copy(j):
        return pltpu.make_async_copy(
            cen_hbm.at[chunk_span(j)], cen.at[chunk_span(j)], cen_sem.at[j]
        )

    own = x * 2 + y
    mine = pltpu.make_async_copy(vec_hbm, rows.at[c, z, own], local_sem.at[0])
    mine.start()
    for j in range(chunks):
        cen_copy(j).start()

    barrier = pltpu.get_barrier_semaphore()
    for o in range(1, cent):
        pl.semaphore_signal(
            barrier, inc=1, device_id=(x, lax.rem(i + o, cent)), device_id_type=MESH
        )
    pl.semaphore_signal(barrier, inc=1, device_id=(1 - x, i), device_id_type=MESH)
    mine.wait()
    pl.semaphore_wait(barrier, cent)

    def slab(o):
        return lax.rem(jnp.where(z < nz // 2, z + o, z + nz - o), nz)

    def remote(piece, send_sem, recv_sem, to):
        return pltpu.make_async_remote_copy(
            src_ref=piece, dst_ref=piece, send_sem=send_sem, recv_sem=recv_sem,
            device_id=to, device_id_type=MESH,
        )

    x_peer = (1 - x, i)
    y_peer = (x, (z * 2 + 1 - y) * 2 + c)

    def over_z(o):
        to = (x, (slab(o) * 2 + y) * 2 + c)
        return remote(rows.at[c, z, own], z_send.at[o], z_recv.at[z], to)

    def over_x(o):
        return remote(rows.at[c, slab(o), own], xy_send.at[0, o], xy_recv.at[0, o], x_peer)

    def over_y(o):
        return remote(rows.at[c, slab(o), own], xy_send.at[1, o], xy_recv.at[1, o], y_peer)

    def arrived(way, o):
        source = jnp.where(way == 0, (1 - x) * 2 + y, x * 2 + 1 - y)
        piece = rows.at[c, slab(o), source]
        return remote(piece, xy_send.at[way, o], xy_recv.at[way, o], x_peer)

    relay_source = jnp.where(c == 0, (1 - x) * 2 + y, x * 2 + 1 - y)
    relay_to = (jnp.where(c == 0, x, 1 - x), jnp.where(c == 0, y_peer[1], i))

    def relay(o):
        return remote(
            rows.at[c, slab(o), relay_source], relay_send.at[o], relay_recv.at[o], relay_to
        )

    def relayed(o):
        piece = rows.at[c, slab(o), (1 - x) * 2 + 1 - y]
        return remote(piece, relay_send.at[o], relay_recv.at[o], relay_to)

    def sibling(o, core):
        to = (x, i + 1 - 2 * c)
        return remote(rows.at[core, slab(o)], sib_send.at[o], sib_recv.at[o], to)

    def z_arrival(o):
        piece = rows.at[c, slab(o), own]
        return remote(piece, z_send.at[o], z_recv.at[slab(o)], y_peer)

    def forward(o):
        if o:
            z_arrival(o).wait_recv()
        over_x(o).start()
        over_y(o).start()

    def pass_on(o):
        arrived(c, o).wait_recv()
        relay(o).start()

    def complete(o):
        arrived(1 - c, o).wait_recv()
        relayed(o).wait_recv()
        sibling(o, c).start()

    def core_of(p):
        return c if p == 0 else 1 - c

    def rows_copy(p):
        return pltpu.make_async_copy(rows.at[core_of(p)], rows_hbm.at[p], local_sem.at[1 + p])

    forward(0)
    for o in range(1, nz):
        over_z(o).start()
    for o in range(1, nz):
        forward(o)
        pass_on(o - 1)
    pass_on(nz - 1)
    for o in range(nz):
        complete(o)

    def score(p, j, peak):
        if p == 0:
            cen_copy(j).wait()
        block = lax.dot_general(
            cen[chunk_span(j)], rows[core_of(p)].reshape(pair, rows.shape[4]), (((1,), (1,)), ((), ())),
            preferred_element_type=jnp.float32,
        )
        scores[chunk_span(j), p * pair : (p + 1) * pair] = block
        return jnp.maximum(peak, jnp.max(block.reshape(-1, 8, pair), axis=0))

    scale = math.log2(math.e) / softness_scale

    def e_copy(j):
        return pltpu.make_async_copy(
            expo.at[chunk_span(j)], e_hbm.at[chunk_span(j)], out_sem.at[j]
        )

    def exponents(p, peak, last):
        columns = slice(p * pair, (p + 1) * pair)

        def whole(j, acc):
            def part(t, acc):
                span = pl.ds(pl.multiple_of(j * SCORE_ROWS + t * EXP_ROWS, EXP_ROWS), EXP_ROWS)
                value = jnp.exp2((scores[span, columns] - peak) * scale)
                expo[span, columns] = value.astype(jnp.bfloat16)
                return acc + jnp.sum(value.reshape(-1, 8, pair), axis=0)

            acc = lax.fori_loop(0, SCORE_ROWS // EXP_ROWS, part, acc)
            if last:
                e_copy(j).start()
            return acc

        acc = lax.fori_loop(0, chunks, whole, jnp.zeros((8, pair), jnp.float32))
        acc = jnp.sum(acc, axis=0, keepdims=True)
        for t in range(per):
            lanes = slice(t * LANES, (t + 1) * LANES)
            at = core_of(p) * per + t
            stats[i, pl.ds(at, 1), :] = peak[:, lanes]
            stats[i, pl.ds(2 * per + at, 1), :] = acc[:, lanes]

    for p in range(2):
        if p:
            for o in range(nz):
                sibling(o, 1 - c).wait_recv()
        rows_copy(p).start()
        peak = jnp.full((8, pair), -jnp.inf, jnp.float32)
        for j in range(chunks):
            peak = score(p, j, peak)
        peak = jnp.max(peak, axis=0, keepdims=True)
        exponents(p, peak, p == 1)

    def stat_copy(o, slot):
        return pltpu.make_async_remote_copy(
            src_ref=stats.at[i], dst_ref=stats.at[slot], send_sem=stat_send.at[o],
            recv_sem=stat_recv.at[o], device_id=(x, lax.rem(i + o, cent)), device_id_type=MESH,
        )

    for o in range(1, cent):
        stat_copy(o, i).start()
    for o in range(1, cent):
        stat_copy(o, lax.rem(i + cent - o, cent)).wait_recv()
    peaks = stats[:, 0 : 2 * per, :]
    highest = jnp.max(peaks, axis=0)
    summed = jnp.sum(stats[:, 2 * per : 4 * per, :] * jnp.exp2((peaks - highest) * scale), axis=0)
    resc[...] = jnp.exp2((stats[i, 0 : 2 * per, :] - highest) * scale) * (mass_scale / summed)
    for p in range(2):
        for t in range(per):
            g = p * per + t
            resc_ref[g : g + 1, :] = resc[pl.ds(core_of(p) * per + t, 1), :]
    for o in range(1, cent):
        stat_copy(o, i).wait_send()
    for o in range(nz):
        if o:
            over_z(o).wait_send()
        over_x(o).wait_send()
        over_y(o).wait_send()
        relay(o).wait_send()
        sibling(o, c).wait_send()
    for p in range(2):
        rows_copy(p).wait()
    for j in range(chunks):
        e_copy(j).wait()


def update_kernel(
    which, e_ref, resc_ref, cen_own, cen_other, rows_own, rows_other, new_ref, loads_ref
):
    j = pl.program_id(0)
    groups = resc_ref.shape[0]
    mass = None
    parts = []
    for g in range(groups):
        lanes = slice(g * LANES, (g + 1) * LANES)
        p = e_ref[:, lanes].astype(jnp.float32) * resc_ref[g : g + 1, :]
        mass = p if mass is None else mass + p
        parts.append(p.astype(jnp.bfloat16))
    weights = jnp.concatenate(parts, axis=1)
    for b in range(mass.shape[0] // LANES):
        block = mass[b * LANES : (b + 1) * LANES].T
        loads_ref[j, b : b + 1, :] = jnp.sum(block, axis=0, keepdims=True)
    own = cen_own[...].astype(jnp.float32) + jnp.dot(
        weights, rows_own[...], preferred_element_type=jnp.float32
    )
    other = cen_other[...].astype(jnp.float32) + jnp.dot(
        weights, rows_other[...], preferred_element_type=jnp.float32
    )
    width = own.shape[1] + other.shape[1]
    square = (
        jnp.sum(own * own, axis=1, keepdims=True) + jnp.sum(other * other, axis=1, keepdims=True)
    ) / width
    new_ref[...] = (own * lax.rsqrt(square + 1e-06)).astype(new_ref.dtype)


def kernel_form(vectors, centroids):
    dp = lax.axis_size("dp")
    cent = lax.axis_size("cent")
    nz = cent // 4
    block_rows, width = vectors.shape
    total = block_rows * dp * cent
    local = centroids.shape[0]
    mass_scale = local * cent / total
    chunks = local // SCORE_ROWS
    groups = total // LANES
    e, rows, resc = pl.pallas_call(
        functools.partial(gather_kernel, cent, nz, mass_scale),
        out_shape=(
            jax.ShapeDtypeStruct((local, total), jnp.bfloat16),
            jax.ShapeDtypeStruct((2, nz, 4, block_rows, width), jnp.bfloat16),
            jax.ShapeDtypeStruct((groups, LANES), jnp.float32),
        ),
        in_specs=[pl.BlockSpec(memory_space=pl.ANY)] * 2,
        out_specs=(
            pl.BlockSpec(memory_space=pl.ANY),
            pl.BlockSpec(memory_space=pl.ANY),
            pl.BlockSpec(memory_space=pltpu.VMEM),
        ),
        scratch_shapes=[
            pltpu.VMEM((local, width), jnp.bfloat16),
            pltpu.VMEM((local, total), jnp.float32),
            pltpu.VMEM((local, total), jnp.bfloat16),
            pltpu.VMEM((2, nz, 4, block_rows, width), jnp.bfloat16),
            pltpu.VMEM((cent, 2 * groups, LANES), jnp.float32),
            pltpu.VMEM((groups, LANES), jnp.float32),
            pltpu.SemaphoreType.DMA((3,)),
            pltpu.SemaphoreType.DMA((chunks,)),
            pltpu.SemaphoreType.DMA((chunks,)),
            pltpu.SemaphoreType.DMA((nz,)),
            pltpu.SemaphoreType.DMA((nz,)),
            pltpu.SemaphoreType.DMA((2, nz)),
            pltpu.SemaphoreType.DMA((2, nz)),
            pltpu.SemaphoreType.DMA((nz,)),
            pltpu.SemaphoreType.DMA((nz,)),
            pltpu.SemaphoreType.DMA((nz,)),
            pltpu.SemaphoreType.DMA((nz,)),
            pltpu.SemaphoreType.DMA((cent,)),
            pltpu.SemaphoreType.DMA((cent,)),
        ],
        compiler_params=pltpu.CompilerParams(
            collective_id=0, has_side_effects=True, vmem_limit_bytes=VMEM_BYTES
        ),
        cost_estimate=pl.CostEstimate(
            flops=2 * local * total * width, bytes_accessed=2 * local * (width + total),
            transcendentals=local * total,
        ),
    )(vectors, centroids)
    rows = rows.reshape(total, width)
    half = width // 2
    steps = local // SUM_ROWS
    which = jnp.reshape(lax.axis_index("dp"), (1,)).astype(jnp.int32)
    new, loads = pl.pallas_call(
        update_kernel,
        out_shape=(
            jax.ShapeDtypeStruct((local, half), jnp.bfloat16),
            jax.ShapeDtypeStruct((steps, SUM_ROWS // LANES, LANES), jnp.float32),
        ),
        grid_spec=pltpu.PrefetchScalarGridSpec(
            num_scalar_prefetch=1,
            grid=(steps,),
            in_specs=[
                pl.BlockSpec((SUM_ROWS, total), lambda j, d: (j, 0)),
                pl.BlockSpec((groups, LANES), lambda j, d: (0, 0)),
                pl.BlockSpec((SUM_ROWS, half), lambda j, d: (j, d[0])),
                pl.BlockSpec((SUM_ROWS, half), lambda j, d: (j, 1 - d[0])),
                pl.BlockSpec((total, half), lambda j, d: (0, d[0])),
                pl.BlockSpec((total, half), lambda j, d: (0, 1 - d[0])),
            ],
            out_specs=(
                pl.BlockSpec((SUM_ROWS, half), lambda j, d: (j, 0)),
                pl.BlockSpec((steps, SUM_ROWS // LANES, LANES), lambda j, d: (0, 0, 0)),
            ),
        ),
        compiler_params=pltpu.CompilerParams(vmem_limit_bytes=VMEM_BYTES),
        cost_estimate=pl.CostEstimate(
            flops=2 * local * total * width, bytes_accessed=2 * local * (width + total + half),
            transcendentals=local,
        ),
    )(which, e, resc, centroids, centroids, rows, rows)
    return (new, loads.reshape(local))


def solution(mesh):
    dp, cent = mesh.shape["dp"], mesh.shape["cent"]

    def on_device(vectors, centroids):
        total = vectors.shape[0] * dp * cent
        fits = (
            dp == 2
            and cent % 8 == 0
            and vectors.shape[0] % 16 == 0
            and total % (2 * LANES) == 0
            and total <= 1024
            and centroids.shape[0] % SCORE_ROWS == 0
            and centroids.shape[0] <= 4096
        )
        return (kernel_form if fits else plain_form)(vectors, centroids)

    placed = (P(("dp", "cent"), None), P("cent", None))
    return jax.shard_map(
        on_device,
        mesh=mesh,
        in_specs=placed,
        out_specs=(P("cent", "dp"), P("cent")),
        check_vma=False,
    )
```

```python
import functools
import math
import jax
import jax.numpy as jnp
from jax import lax
from jax.experimental import pallas as pl
from jax.experimental.pallas import tpu as pltpu
from jax.sharding import PartitionSpec as P

softness_scale = 0.1
MESH = pl.DeviceIdType.MESH
LANES = 128
SCORE_ROWS = 1024
SUM_ROWS = 1024
EXP_ROWS = 64
VMEM_BYTES = 56 * 1024 * 1024


def plain_form(vectors, centroids):
    dp = lax.axis_size("dp")
    cent = lax.axis_size("cent")
    total_rows = vectors.shape[0] * dp * cent
    mass_scale = centroids.shape[0] * cent / total_rows
    rows = lax.all_gather(vectors, ("dp", "cent"), axis=0, tiled=True)
    scores = (
        lax.dot_general(
            centroids, rows, (((1,), (1,)), ((), ())), preferred_element_type=jnp.float32
        )
        / softness_scale
    )
    local_peak = jnp.max(scores, axis=0)
    exponent = jnp.exp(scores - local_peak[None, :])
    local_sum = jnp.sum(exponent, axis=0)
    stats = lax.all_gather(jnp.stack([local_peak, local_sum]), "cent", axis=0)
    highest = jnp.max(stats[:, 0], axis=0)
    summed = jnp.sum(stats[:, 1] * jnp.exp(stats[:, 0] - highest[None, :]), axis=0)
    rescale = jnp.exp(local_peak - highest) / summed
    probability = exponent * rescale[None, :]
    weights = probability.astype(jnp.bfloat16)
    loads = jnp.sum(probability, axis=1) * mass_scale
    sums = lax.dot_general(
        weights, rows, (((1,), (0,)), ((), ())), preferred_element_type=jnp.float32
    )
    shifted = centroids.astype(jnp.float32) + sums * mass_scale
    factor = lax.rsqrt(jnp.mean(shifted * shifted, axis=1, keepdims=True) + 1e-06)
    columns = centroids.shape[1] // dp
    own = lax.dynamic_slice_in_dim(shifted, lax.axis_index("dp") * columns, columns, 1)
    return ((own * factor).astype(jnp.bfloat16), loads)


def gather_kernel(
    cent, nz, mass_scale, vec_hbm, cen_hbm, e_hbm, rows_hbm, resc_ref,
    cen, scores, expo, rows, stats, resc,
    local_sem, cen_sem, out_sem, z_send, z_recv, xy_send, xy_recv, relay_send, relay_recv,
    sib_send, sib_recv, stat_send, stat_recv,
):
    x = lax.axis_index("dp")
    i = lax.axis_index("cent")
    c = i % 2
    y = (i // 2) % 2
    z = i // 4
    total = scores.shape[1]
    pair = 2 * LANES
    chunks = cen_hbm.shape[0] // SCORE_ROWS

    def chunk_span(j):
        return pl.ds(pl.multiple_of(j * SCORE_ROWS, SCORE_ROWS), SCORE_ROWS)

    def cen_copy(j):
        return pltpu.make_async_copy(
            cen_hbm.at[chunk_span(j)], cen.at[chunk_span(j)], cen_sem.at[j]
        )

    own = x * 2 + y
    mine = pltpu.make_async_copy(vec_hbm, rows.at[z, c, own], local_sem.at[0])
    mine.start()
    for j in range(chunks):
        cen_copy(j).start()

    barrier = pltpu.get_barrier_semaphore()
    for o in range(1, cent):
        pl.semaphore_signal(
            barrier, inc=1, device_id=(x, lax.rem(i + o, cent)), device_id_type=MESH
        )
    pl.semaphore_signal(barrier, inc=1, device_id=(1 - x, i), device_id_type=MESH)
    mine.wait()
    pl.semaphore_wait(barrier, cent)

    def slab(o):
        return lax.rem(jnp.where(z < nz // 2, z + o, z + nz - o), nz)

    def remote(piece, send_sem, recv_sem, to):
        return pltpu.make_async_remote_copy(
            src_ref=piece, dst_ref=piece, send_sem=send_sem, recv_sem=recv_sem,
            device_id=to, device_id_type=MESH,
        )

    x_peer = (1 - x, i)
    y_peer = (x, (z * 2 + 1 - y) * 2 + c)

    def over_z(o):
        to = (x, (slab(o) * 2 + y) * 2 + c)
        return remote(rows.at[z, c, own], z_send.at[o], z_recv.at[z], to)

    def over_x(o):
        return remote(rows.at[slab(o), c, own], xy_send.at[0, o], xy_recv.at[0, o], x_peer)

    def over_y(o):
        return remote(rows.at[slab(o), c, own], xy_send.at[1, o], xy_recv.at[1, o], y_peer)

    def arrived(way, o):
        source = jnp.where(way == 0, (1 - x) * 2 + y, x * 2 + 1 - y)
        piece = rows.at[slab(o), c, source]
        return remote(piece, xy_send.at[way, o], xy_recv.at[way, o], x_peer)

    relay_source = jnp.where(c == 0, (1 - x) * 2 + y, x * 2 + 1 - y)
    relay_to = (jnp.where(c == 0, x, 1 - x), jnp.where(c == 0, y_peer[1], i))

    def relay(o):
        return remote(
            rows.at[slab(o), c, relay_source], relay_send.at[o], relay_recv.at[o], relay_to
        )

    def relayed(o):
        piece = rows.at[slab(o), c, (1 - x) * 2 + 1 - y]
        return remote(piece, relay_send.at[o], relay_recv.at[o], relay_to)

    def sibling(o, core):
        to = (x, i + 1 - 2 * c)
        return remote(rows.at[slab(o), core], sib_send.at[o], sib_recv.at[o], to)

    def z_arrival(o):
        piece = rows.at[slab(o), c, own]
        return remote(piece, z_send.at[o], z_recv.at[slab(o)], y_peer)

    def forward(o):
        if o:
            z_arrival(o).wait_recv()
        over_x(o).start()
        over_y(o).start()

    def pass_on(o):
        arrived(c, o).wait_recv()
        relay(o).start()

    def complete(o):
        arrived(1 - c, o).wait_recv()
        relayed(o).wait_recv()
        sibling(o, c).start()

    def rows_copy(o):
        return pltpu.make_async_copy(rows.at[slab(o)], rows_hbm.at[o], local_sem.at[1 + o])

    def usable(o):
        sibling(o, 1 - c).wait_recv()
        rows_copy(o).start()

    forward(0)
    for o in range(1, nz):
        over_z(o).start()
    for o in range(1, nz):
        forward(o)
        pass_on(o - 1)
        if o >= nz - 2:
            complete(o - nz + 2)

    def score(p, j, peak):
        if p == 0:
            cen_copy(j).wait()
        two = [rows[slab(2 * p + t)].reshape(LANES, rows.shape[4]) for t in range(2)]
        block = lax.dot_general(
            cen[chunk_span(j)], jnp.concatenate(two, axis=0), (((1,), (1,)), ((), ())),
            preferred_element_type=jnp.float32,
        )
        scores[chunk_span(j), p * pair : (p + 1) * pair] = block
        return jnp.maximum(peak, jnp.max(block.reshape(-1, 8, pair), axis=0))

    scale = math.log2(math.e) / softness_scale

    def e_copy(j):
        return pltpu.make_async_copy(
            expo.at[chunk_span(j)], e_hbm.at[chunk_span(j)], out_sem.at[j]
        )

    def exponents(p, peak, last):
        columns = slice(p * pair, (p + 1) * pair)

        def whole(j, acc):
            def part(t, acc):
                span = pl.ds(pl.multiple_of(j * SCORE_ROWS + t * EXP_ROWS, EXP_ROWS), EXP_ROWS)
                value = jnp.exp2((scores[span, columns] - peak) * scale)
                expo[span, columns] = value.astype(jnp.bfloat16)
                return acc + jnp.sum(value.reshape(-1, 8, pair), axis=0)

            acc = lax.fori_loop(0, SCORE_ROWS // EXP_ROWS, part, acc)
            if last:
                e_copy(j).start()
            return acc

        acc = lax.fori_loop(0, chunks, whole, jnp.zeros((8, pair), jnp.float32))
        acc = jnp.sum(acc, axis=0, keepdims=True)
        for t in range(2):
            lanes = slice(t * LANES, (t + 1) * LANES)
            at = slab(2 * p + t)
            stats[i, pl.ds(at, 1), :] = peak[:, lanes]
            stats[i, pl.ds(nz + at, 1), :] = acc[:, lanes]

    later = [functools.partial(pass_on, nz - 1)]
    later += [functools.partial(complete, o) for o in range(2, nz)]
    for p in range(nz // 2):
        for t in range(2):
            usable(2 * p + t)
        peak = jnp.full((8, pair), -jnp.inf, jnp.float32)
        for j in range(chunks):
            peak = score(p, j, peak)
            if later:
                later.pop(0)()
        while later:
            later.pop(0)()
        peak = jnp.max(peak, axis=0, keepdims=True)
        exponents(p, peak, p == nz // 2 - 1)

    def stat_copy(o, slot):
        return pltpu.make_async_remote_copy(
            src_ref=stats.at[i], dst_ref=stats.at[slot], send_sem=stat_send.at[o],
            recv_sem=stat_recv.at[o], device_id=(x, lax.rem(i + o, cent)), device_id_type=MESH,
        )

    for o in range(1, cent):
        stat_copy(o, i).start()
    for o in range(1, cent):
        stat_copy(o, lax.rem(i + cent - o, cent)).wait_recv()
    peaks = stats[:, 0:nz, :]
    highest = jnp.max(peaks, axis=0)
    summed = jnp.sum(stats[:, nz : 2 * nz, :] * jnp.exp2((peaks - highest) * scale), axis=0)
    resc[...] = jnp.exp2((stats[i, 0:nz, :] - highest) * scale) * (mass_scale / summed)
    for o in range(nz):
        resc_ref[o : o + 1, :] = resc[pl.ds(slab(o), 1), :]
    for o in range(1, cent):
        stat_copy(o, i).wait_send()
    for o in range(nz):
        if o:
            over_z(o).wait_send()
        over_x(o).wait_send()
        over_y(o).wait_send()
        relay(o).wait_send()
        sibling(o, c).wait_send()
        rows_copy(o).wait()
    for j in range(chunks):
        e_copy(j).wait()


def update_kernel(
    which, e_ref, resc_ref, cen_own, cen_other, rows_own, rows_other, new_ref, loads_ref
):
    j = pl.program_id(0)
    groups = resc_ref.shape[0]
    mass = None
    parts = []
    for g in range(groups):
        lanes = slice(g * LANES, (g + 1) * LANES)
        p = e_ref[:, lanes].astype(jnp.float32) * resc_ref[g : g + 1, :]
        mass = p if mass is None else mass + p
        parts.append(p.astype(jnp.bfloat16))
    weights = jnp.concatenate(parts, axis=1)
    for b in range(mass.shape[0] // LANES):
        block = mass[b * LANES : (b + 1) * LANES].T
        loads_ref[j, b : b + 1, :] = jnp.sum(block, axis=0, keepdims=True)
    own = cen_own[...].astype(jnp.float32) + jnp.dot(
        weights, rows_own[...], preferred_element_type=jnp.float32
    )
    other = cen_other[...].astype(jnp.float32) + jnp.dot(
        weights, rows_other[...], preferred_element_type=jnp.float32
    )
    width = own.shape[1] + other.shape[1]
    square = (
        jnp.sum(own * own, axis=1, keepdims=True) + jnp.sum(other * other, axis=1, keepdims=True)
    ) / width
    new_ref[...] = (own * lax.rsqrt(square + 1e-06)).astype(new_ref.dtype)


def kernel_form(vectors, centroids):
    dp = lax.axis_size("dp")
    cent = lax.axis_size("cent")
    nz = cent // 4
    block_rows, width = vectors.shape
    total = block_rows * dp * cent
    local = centroids.shape[0]
    mass_scale = local * cent / total
    chunks = local // SCORE_ROWS
    groups = total // LANES
    e, rows, resc = pl.pallas_call(
        functools.partial(gather_kernel, cent, nz, mass_scale),
        out_shape=(
            jax.ShapeDtypeStruct((local, total), jnp.bfloat16),
            jax.ShapeDtypeStruct((nz, 2, 4, block_rows, width), jnp.bfloat16),
            jax.ShapeDtypeStruct((groups, LANES), jnp.float32),
        ),
        in_specs=[pl.BlockSpec(memory_space=pl.ANY)] * 2,
        out_specs=(
            pl.BlockSpec(memory_space=pl.ANY),
            pl.BlockSpec(memory_space=pl.ANY),
            pl.BlockSpec(memory_space=pltpu.VMEM),
        ),
        scratch_shapes=[
            pltpu.VMEM((local, width), jnp.bfloat16),
            pltpu.VMEM((local, total), jnp.float32),
            pltpu.VMEM((local, total), jnp.bfloat16),
            pltpu.VMEM((nz, 2, 4, block_rows, width), jnp.bfloat16),
            pltpu.VMEM((cent, 2 * groups, LANES), jnp.float32),
            pltpu.VMEM((groups, LANES), jnp.float32),
            pltpu.SemaphoreType.DMA((1 + nz,)),
            pltpu.SemaphoreType.DMA((chunks,)),
            pltpu.SemaphoreType.DMA((chunks,)),
            pltpu.SemaphoreType.DMA((nz,)),
            pltpu.SemaphoreType.DMA((nz,)),
            pltpu.SemaphoreType.DMA((2, nz)),
            pltpu.SemaphoreType.DMA((2, nz)),
            pltpu.SemaphoreType.DMA((nz,)),
            pltpu.SemaphoreType.DMA((nz,)),
            pltpu.SemaphoreType.DMA((nz,)),
            pltpu.SemaphoreType.DMA((nz,)),
            pltpu.SemaphoreType.DMA((cent,)),
            pltpu.SemaphoreType.DMA((cent,)),
        ],
        compiler_params=pltpu.CompilerParams(
            collective_id=0, has_side_effects=True, vmem_limit_bytes=VMEM_BYTES
        ),
        cost_estimate=pl.CostEstimate(
            flops=2 * local * total * width, bytes_accessed=2 * local * (width + total),
            transcendentals=local * total,
        ),
    )(vectors, centroids)
    rows = rows.reshape(total, width)
    half = width // 2
    steps = local // SUM_ROWS
    which = jnp.reshape(lax.axis_index("dp"), (1,)).astype(jnp.int32)
    new, loads = pl.pallas_call(
        update_kernel,
        out_shape=(
            jax.ShapeDtypeStruct((local, half), jnp.bfloat16),
            jax.ShapeDtypeStruct((steps, SUM_ROWS // LANES, LANES), jnp.float32),
        ),
        grid_spec=pltpu.PrefetchScalarGridSpec(
            num_scalar_prefetch=1,
            grid=(steps,),
            in_specs=[
                pl.BlockSpec((SUM_ROWS, total), lambda j, d: (j, 0)),
                pl.BlockSpec((groups, LANES), lambda j, d: (0, 0)),
                pl.BlockSpec((SUM_ROWS, half), lambda j, d: (j, d[0])),
                pl.BlockSpec((SUM_ROWS, half), lambda j, d: (j, 1 - d[0])),
                pl.BlockSpec((total, half), lambda j, d: (0, d[0])),
                pl.BlockSpec((total, half), lambda j, d: (0, 1 - d[0])),
            ],
            out_specs=(
                pl.BlockSpec((SUM_ROWS, half), lambda j, d: (j, 0)),
                pl.BlockSpec((steps, SUM_ROWS // LANES, LANES), lambda j, d: (0, 0, 0)),
            ),
        ),
        compiler_params=pltpu.CompilerParams(vmem_limit_bytes=VMEM_BYTES),
        cost_estimate=pl.CostEstimate(
            flops=2 * local * total * width, bytes_accessed=2 * local * (width + total + half),
            transcendentals=local,
        ),
    )(which, e, resc, centroids, centroids, rows, rows)
    return (new, loads.reshape(local))


def solution(mesh):
    dp, cent = mesh.shape["dp"], mesh.shape["cent"]

    def on_device(vectors, centroids):
        total = vectors.shape[0] * dp * cent
        fits = (
            dp == 2
            and cent % 8 == 0
            and vectors.shape[0] * 8 == LANES
            and total <= 1024
            and centroids.shape[0] % SCORE_ROWS == 0
            and centroids.shape[0] <= 4096
        )
        return (kernel_form if fits else plain_form)(vectors, centroids)

    placed = (P(("dp", "cent"), None), P("cent", None))
    return jax.shard_map(
        on_device,
        mesh=mesh,
        in_specs=placed,
        out_specs=(P("cent", "dp"), P("cent")),
        check_vma=False,
    )
```

```python
import functools
import math
import jax
import jax.numpy as jnp
from jax import lax
from jax.experimental import pallas as pl
from jax.experimental.pallas import tpu as pltpu
from jax.sharding import PartitionSpec as P

softness_scale = 0.1
MESH = pl.DeviceIdType.MESH
LANES = 128
SCORE_ROWS = 1024
SUM_ROWS = 1024
PIECE_ROWS = 512
EXP_ROWS = 64
VMEM_BYTES = 56 * 1024 * 1024


def plain_form(vectors, centroids):
    dp = lax.axis_size("dp")
    cent = lax.axis_size("cent")
    total_rows = vectors.shape[0] * dp * cent
    mass_scale = centroids.shape[0] * cent / total_rows
    rows = lax.all_gather(vectors, ("dp", "cent"), axis=0, tiled=True)
    scores = (
        lax.dot_general(
            centroids, rows, (((1,), (1,)), ((), ())), preferred_element_type=jnp.float32
        )
        / softness_scale
    )
    local_peak = jnp.max(scores, axis=0)
    exponent = jnp.exp(scores - local_peak[None, :])
    local_sum = jnp.sum(exponent, axis=0)
    stats = lax.all_gather(jnp.stack([local_peak, local_sum]), "cent", axis=0)
    highest = jnp.max(stats[:, 0], axis=0)
    summed = jnp.sum(stats[:, 1] * jnp.exp(stats[:, 0] - highest[None, :]), axis=0)
    rescale = jnp.exp(local_peak - highest) / summed
    probability = exponent * rescale[None, :]
    weights = probability.astype(jnp.bfloat16)
    loads = jnp.sum(probability, axis=1) * mass_scale
    sums = lax.dot_general(
        weights, rows, (((1,), (0,)), ((), ())), preferred_element_type=jnp.float32
    )
    shifted = centroids.astype(jnp.float32) + sums * mass_scale
    factor = lax.rsqrt(jnp.mean(shifted * shifted, axis=1, keepdims=True) + 1e-06)
    columns = centroids.shape[1] // dp
    own = lax.dynamic_slice_in_dim(shifted, lax.axis_index("dp") * columns, columns, 1)
    return ((own * factor).astype(jnp.bfloat16), loads)


def gather_kernel(
    cent, nz, mass_scale, vec_hbm, cen_hbm, e_hbm, rows_hbm, resc_ref,
    cen, scores, expo, rows, stats, resc,
    local_sem, cen_sem, out_sem, z_send, z_recv, xy_send, xy_recv, relay_send, relay_recv,
    sib_send, sib_recv, stat_send, stat_recv,
):
    x = lax.axis_index("dp")
    i = lax.axis_index("cent")
    c = i % 2
    y = (i // 2) % 2
    z = i // 4
    total = scores.shape[1]
    pair = 2 * LANES
    chunks = cen_hbm.shape[0] // SCORE_ROWS

    def chunk_span(j):
        return pl.ds(pl.multiple_of(j * SCORE_ROWS, SCORE_ROWS), SCORE_ROWS)

    def cen_copy(j):
        return pltpu.make_async_copy(
            cen_hbm.at[chunk_span(j)], cen.at[chunk_span(j)], cen_sem.at[j]
        )

    own = x * 2 + y
    mine = pltpu.make_async_copy(vec_hbm, rows.at[z, c, own], local_sem.at[0])
    mine.start()
    for j in range(chunks):
        cen_copy(j).start()

    barrier = pltpu.get_barrier_semaphore()
    for o in range(1, cent):
        pl.semaphore_signal(
            barrier, inc=1, device_id=(x, lax.rem(i + o, cent)), device_id_type=MESH
        )
    pl.semaphore_signal(barrier, inc=1, device_id=(1 - x, i), device_id_type=MESH)
    mine.wait()
    pl.semaphore_wait(barrier, cent)

    def slab(o):
        return lax.rem(jnp.where(z < nz // 2, z + o, z + nz - o), nz)

    def remote(piece, send_sem, recv_sem, to):
        return pltpu.make_async_remote_copy(
            src_ref=piece, dst_ref=piece, send_sem=send_sem, recv_sem=recv_sem,
            device_id=to, device_id_type=MESH,
        )

    x_peer = (1 - x, i)
    y_peer = (x, (z * 2 + 1 - y) * 2 + c)

    def over_z(o):
        to = (x, (slab(o) * 2 + y) * 2 + c)
        return remote(rows.at[z, c, own], z_send.at[o], z_recv.at[z], to)

    def over_x(o):
        return remote(rows.at[slab(o), c, own], xy_send.at[0, o], xy_recv.at[0, o], x_peer)

    def over_y(o):
        return remote(rows.at[slab(o), c, own], xy_send.at[1, o], xy_recv.at[1, o], y_peer)

    def arrived(way, o):
        source = jnp.where(way == 0, (1 - x) * 2 + y, x * 2 + 1 - y)
        piece = rows.at[slab(o), c, source]
        return remote(piece, xy_send.at[way, o], xy_recv.at[way, o], x_peer)

    relay_source = jnp.where(c == 0, (1 - x) * 2 + y, x * 2 + 1 - y)
    relay_to = (jnp.where(c == 0, x, 1 - x), jnp.where(c == 0, y_peer[1], i))

    def relay(o):
        return remote(
            rows.at[slab(o), c, relay_source], relay_send.at[o], relay_recv.at[o], relay_to
        )

    def relayed(o):
        piece = rows.at[slab(o), c, (1 - x) * 2 + 1 - y]
        return remote(piece, relay_send.at[o], relay_recv.at[o], relay_to)

    def sibling(o, core):
        to = (x, i + 1 - 2 * c)
        return remote(rows.at[slab(o), core], sib_send.at[o], sib_recv.at[o], to)

    def z_arrival(o):
        piece = rows.at[slab(o), c, own]
        return remote(piece, z_send.at[o], z_recv.at[slab(o)], y_peer)

    def forward(o):
        if o:
            z_arrival(o).wait_recv()
        over_x(o).start()
        over_y(o).start()

    def pass_on(o):
        arrived(c, o).wait_recv()
        relay(o).start()

    def complete(o):
        arrived(1 - c, o).wait_recv()
        relayed(o).wait_recv()
        sibling(o, c).start()

    def rows_copy(o):
        return pltpu.make_async_copy(rows.at[slab(o)], rows_hbm.at[o], local_sem.at[1 + o])

    def usable(o):
        sibling(o, 1 - c).wait_recv()
        rows_copy(o).start()

    forward(0)
    for o in range(1, nz):
        over_z(o).start()
    for o in range(1, nz):
        forward(o)
        pass_on(o - 1)
        if o >= nz - 2:
            complete(o - nz + 2)

    def score(p, j, peak):
        if p == 0:
            cen_copy(j).wait()
        two = [rows[slab(2 * p + t)].reshape(LANES, rows.shape[4]) for t in range(2)]
        block = lax.dot_general(
            cen[chunk_span(j)], jnp.concatenate(two, axis=0), (((1,), (1,)), ((), ())),
            preferred_element_type=jnp.float32,
        )
        scores[chunk_span(j), p * pair : (p + 1) * pair] = block
        return jnp.maximum(peak, jnp.max(block.reshape(-1, 8, pair), axis=0))

    scale = math.log2(math.e) / softness_scale

    def e_copy(j):
        return pltpu.make_async_copy(
            expo.at[chunk_span(j)], e_hbm.at[chunk_span(j)], out_sem.at[j]
        )

    def exponents(p, peak, last):
        columns = slice(p * pair, (p + 1) * pair)

        def whole(j, acc):
            def part(t, acc):
                span = pl.ds(pl.multiple_of(j * SCORE_ROWS + t * EXP_ROWS, EXP_ROWS), EXP_ROWS)
                value = jnp.exp2((scores[span, columns] - peak) * scale)
                expo[span, columns] = value.astype(jnp.bfloat16)
                return acc + jnp.sum(value.reshape(-1, 8, pair), axis=0)

            acc = lax.fori_loop(0, SCORE_ROWS // EXP_ROWS, part, acc)
            if last:
                e_copy(j).start()
            return acc

        acc = lax.fori_loop(0, chunks, whole, jnp.zeros((8, pair), jnp.float32))
        acc = jnp.sum(acc, axis=0, keepdims=True)
        for t in range(2):
            lanes = slice(t * LANES, (t + 1) * LANES)
            at = slab(2 * p + t)
            stats[i, pl.ds(at, 1), :] = peak[:, lanes]
            stats[i, pl.ds(nz + at, 1), :] = acc[:, lanes]

    later = [functools.partial(pass_on, nz - 1)]
    later += [functools.partial(complete, o) for o in range(2, nz)]
    for p in range(nz // 2):
        for t in range(2):
            usable(2 * p + t)
        peak = jnp.full((8, pair), -jnp.inf, jnp.float32)
        for j in range(chunks):
            peak = score(p, j, peak)
            if later:
                later.pop(0)()
        while later:
            later.pop(0)()
        peak = jnp.max(peak, axis=0, keepdims=True)
        exponents(p, peak, p == nz // 2 - 1)

    def stat_copy(o, slot):
        return pltpu.make_async_remote_copy(
            src_ref=stats.at[i], dst_ref=stats.at[slot], send_sem=stat_send.at[o],
            recv_sem=stat_recv.at[o], device_id=(x, lax.rem(i + o, cent)), device_id_type=MESH,
        )

    for o in range(1, cent):
        stat_copy(o, i).start()
    for o in range(1, cent):
        stat_copy(o, lax.rem(i + cent - o, cent)).wait_recv()
    peaks = stats[:, 0:nz, :]
    highest = jnp.max(peaks, axis=0)
    summed = jnp.sum(stats[:, nz : 2 * nz, :] * jnp.exp2((peaks - highest) * scale), axis=0)
    resc[...] = jnp.exp2((stats[i, 0:nz, :] - highest) * scale) * (mass_scale / summed)
    for o in range(nz):
        resc_ref[o : o + 1, :] = resc[pl.ds(slab(o), 1), :]
    for o in range(1, cent):
        stat_copy(o, i).wait_send()
    for o in range(nz):
        if o:
            over_z(o).wait_send()
        over_x(o).wait_send()
        over_y(o).wait_send()
        relay(o).wait_send()
        sibling(o, c).wait_send()
        rows_copy(o).wait()
    for j in range(chunks):
        e_copy(j).wait()


def update_kernel(
    which, e_ref, resc_ref, cen_own, cen_other, rows_own, rows_other, new_ref, loads_ref
):
    j = pl.program_id(0)
    groups = resc_ref.shape[0]
    width = cen_own.shape[1] + cen_other.shape[1]
    for start in range(0, SUM_ROWS, PIECE_ROWS):
        span = slice(start, start + PIECE_ROWS)
        mass = None
        parts = []
        for g in range(groups):
            lanes = slice(g * LANES, (g + 1) * LANES)
            p = e_ref[span, lanes].astype(jnp.float32) * resc_ref[g : g + 1, :]
            mass = p if mass is None else mass + p
            parts.append(p.astype(jnp.bfloat16))
        weights = jnp.concatenate(parts, axis=1)
        for b in range(PIECE_ROWS // LANES):
            block = mass[b * LANES : (b + 1) * LANES].T
            at = start // LANES + b
            loads_ref[j, at : at + 1, :] = jnp.sum(block, axis=0, keepdims=True)
        own = cen_own[span].astype(jnp.float32) + jnp.dot(
            weights, rows_own[...], preferred_element_type=jnp.float32
        )
        other = cen_other[span].astype(jnp.float32) + jnp.dot(
            weights, rows_other[...], preferred_element_type=jnp.float32
        )
        square = (
            jnp.sum(own * own, axis=1, keepdims=True)
            + jnp.sum(other * other, axis=1, keepdims=True)
        ) / width
        new_ref[span] = (own * lax.rsqrt(square + 1e-06)).astype(new_ref.dtype)


def kernel_form(vectors, centroids):
    dp = lax.axis_size("dp")
    cent = lax.axis_size("cent")
    nz = cent // 4
    block_rows, width = vectors.shape
    total = block_rows * dp * cent
    local = centroids.shape[0]
    mass_scale = local * cent / total
    chunks = local // SCORE_ROWS
    groups = total // LANES
    e, rows, resc = pl.pallas_call(
        functools.partial(gather_kernel, cent, nz, mass_scale),
        out_shape=(
            jax.ShapeDtypeStruct((local, total), jnp.bfloat16),
            jax.ShapeDtypeStruct((nz, 2, 4, block_rows, width), jnp.bfloat16),
            jax.ShapeDtypeStruct((groups, LANES), jnp.float32),
        ),
        in_specs=[pl.BlockSpec(memory_space=pl.ANY)] * 2,
        out_specs=(
            pl.BlockSpec(memory_space=pl.ANY),
            pl.BlockSpec(memory_space=pl.ANY),
            pl.BlockSpec(memory_space=pltpu.VMEM),
        ),
        scratch_shapes=[
            pltpu.VMEM((local, width), jnp.bfloat16),
            pltpu.VMEM((local, total), jnp.float32),
            pltpu.VMEM((local, total), jnp.bfloat16),
            pltpu.VMEM((nz, 2, 4, block_rows, width), jnp.bfloat16),
            pltpu.VMEM((cent, 2 * groups, LANES), jnp.float32),
            pltpu.VMEM((groups, LANES), jnp.float32),
            pltpu.SemaphoreType.DMA((1 + nz,)),
            pltpu.SemaphoreType.DMA((chunks,)),
            pltpu.SemaphoreType.DMA((chunks,)),
            pltpu.SemaphoreType.DMA((nz,)),
            pltpu.SemaphoreType.DMA((nz,)),
            pltpu.SemaphoreType.DMA((2, nz)),
            pltpu.SemaphoreType.DMA((2, nz)),
            pltpu.SemaphoreType.DMA((nz,)),
            pltpu.SemaphoreType.DMA((nz,)),
            pltpu.SemaphoreType.DMA((nz,)),
            pltpu.SemaphoreType.DMA((nz,)),
            pltpu.SemaphoreType.DMA((cent,)),
            pltpu.SemaphoreType.DMA((cent,)),
        ],
        compiler_params=pltpu.CompilerParams(
            collective_id=0, has_side_effects=True, vmem_limit_bytes=VMEM_BYTES
        ),
        cost_estimate=pl.CostEstimate(
            flops=2 * local * total * width, bytes_accessed=2 * local * (width + total),
            transcendentals=local * total,
        ),
    )(vectors, centroids)
    rows = rows.reshape(total, width)
    half = width // 2
    steps = local // SUM_ROWS
    which = jnp.reshape(lax.axis_index("dp"), (1,)).astype(jnp.int32)
    new, loads = pl.pallas_call(
        update_kernel,
        out_shape=(
            jax.ShapeDtypeStruct((local, half), jnp.bfloat16),
            jax.ShapeDtypeStruct((steps, SUM_ROWS // LANES, LANES), jnp.float32),
        ),
        grid_spec=pltpu.PrefetchScalarGridSpec(
            num_scalar_prefetch=1,
            grid=(steps,),
            in_specs=[
                pl.BlockSpec((SUM_ROWS, total), lambda j, d: (j, 0)),
                pl.BlockSpec((groups, LANES), lambda j, d: (0, 0)),
                pl.BlockSpec((SUM_ROWS, half), lambda j, d: (j, d[0])),
                pl.BlockSpec((SUM_ROWS, half), lambda j, d: (j, 1 - d[0])),
                pl.BlockSpec((total, half), lambda j, d: (0, d[0])),
                pl.BlockSpec((total, half), lambda j, d: (0, 1 - d[0])),
            ],
            out_specs=(
                pl.BlockSpec((SUM_ROWS, half), lambda j, d: (j, 0)),
                pl.BlockSpec((steps, SUM_ROWS // LANES, LANES), lambda j, d: (0, 0, 0)),
            ),
        ),
        compiler_params=pltpu.CompilerParams(vmem_limit_bytes=VMEM_BYTES),
        cost_estimate=pl.CostEstimate(
            flops=2 * local * total * width, bytes_accessed=2 * local * (width + total + half),
            transcendentals=local,
        ),
    )(which, e, resc, centroids, centroids, rows, rows)
    return (new, loads.reshape(local))


def solution(mesh):
    dp, cent = mesh.shape["dp"], mesh.shape["cent"]

    def on_device(vectors, centroids):
        total = vectors.shape[0] * dp * cent
        fits = (
            dp == 2
            and cent % 8 == 0
            and vectors.shape[0] * 8 == LANES
            and total <= 1024
            and centroids.shape[0] % SCORE_ROWS == 0
            and centroids.shape[0] <= 4096
        )
        return (kernel_form if fits else plain_form)(vectors, centroids)

    placed = (P(("dp", "cent"), None), P("cent", None))
    return jax.shard_map(
        on_device,
        mesh=mesh,
        in_specs=placed,
        out_specs=(P("cent", "dp"), P("cent")),
        check_vma=False,
    )
```
